32 devices in a mesh: ep: 16 (over z, y, core), dp: 2 (over x).
Axes of the slice: x: 2, y: 2, z: 4, core: 2. Of those that a mesh axis runs over, the one named last changes fastest.
Arguments:
- tokens: bfloat16 [128, 7168], P('ep', 'dp'), may hold values from -6 to 6
- cotangent: bfloat16 [128, 7168], P('ep', 'dp'), may hold values from -6 to 6
- routes: int32 [128, 8], P('ep'), may hold values from 0 to 15, all different within a row; in each aligned block of 8 rows (0 to 7, 8 to 15, ...) at most 8 rows name the same one
- route_weights: float32 [128, 8], P('ep'), may hold values from 0.05 to 0.5
- gate_up: bfloat16 [16, 7168, 4096], P('ep', 'dp'), may hold values from -0.0625 to 0.0625
- down_proj: bfloat16 [16, 2048, 7168], P('ep', None, 'dp'), may hold values from -0.125 to 0.125
Outputs:
- mixed: bfloat16 [128, 7168], P('ep', 'dp')
- token_grad: bfloat16 [128, 7168], P('ep', 'dp')
- gate_up_grad: bfloat16 [16, 7168, 4096], P('ep', 'dp')
The draws below stay inside these ranges and needn't reach their ends.
Inputs may be any that keep to these rules, and one draw needn't show every extreme that they name: `routes`: each token names 8 different experts. The 8 tokens of one index of ep (aligned blocks of rows) name any one expert at most 8 times, a bound that some block reaches.
All inputs are finite; a program needn't handle non-finite values.
Results may differ from the reference program's by a relative error of at most 0.015.
Values may be sent and summed in bfloat16 or wider, within the bound.
A program may use at most 192 MiB of HBM per device.

```python
import math
import jax
import jax.numpy as jnp
import numpy as np
from jax import lax

D = 7168
FF = 2048
TOPK = 8
TOK_DEV = 8
SPLIT = 1
EXPERTS = 16
CAP = 8
TOKENS = 128
N_EP = 16
N_DP = 2


def block_scale(own_key, extent, shards, low, largest):
    def one(dim, blocks):
        steps = jax.random.uniform(jax.random.fold_in(jax.random.fold_in(own_key, 6), dim), (blocks,), jnp.float32, low / len(shards), largest / len(shards))
        return jnp.repeat(jnp.exp(steps), extent[dim] // blocks).reshape((-1,) + (1,) * (len(extent) - dim - 1))

    gain = one(*shards[0])
    for cut in shards[1:]:
        gain = gain * one(*cut)
    return gain


def assign_block(rng, own, number, rows, number_of, top, bound, lean):
    sequence = jax.random.permutation(rng, number_of)
    crowded, common = shares(number_of, rows * top, bound, lean, True), shares(number_of, rows * top, bound, lean, False)
    places = jnp.arange(number_of)

    def named(lengths, rotation):
        used = int((lengths > 0).sum())
        fixed = max(1, used // 4)
        passed = fixed + (places - fixed + rotation * (used - fixed)) % max(1, number_of - fixed)
        return jnp.zeros((number_of,), jnp.int32).at[sequence[jnp.where(places < fixed, places, passed)]].set(jnp.asarray(lengths, jnp.int32))

    lengths = jnp.where(number % 4 == 0, named(crowded, number // 4), named(common, number - number // 4 - 1))
    mixed = jax.random.permutation(jax.random.fold_in(own, 3), number_of)
    donor, receiver = mixed[0:number_of // 2 * 2:2], mixed[1:number_of // 2 * 2:2]
    margin = jnp.minimum(lengths[donor] - 1, bound - lengths[receiver]) // 2
    margin = jnp.where((donor == sequence[0]) | (receiver == sequence[0]) | (lengths[receiver] == 0), 0, jnp.maximum(margin, 0))
    passed = jax.random.randint(jax.random.fold_in(own, 4), (number_of // 2,), 0, 1 << 20) % (margin + 1)
    lengths = lengths.at[donor].add(-passed).at[receiver].add(passed)
    items = jnp.searchsorted(jnp.cumsum(lengths), jnp.arange(rows * top), side="right").astype(jnp.int32)
    table = items.reshape(top, rows).T
    table = table[jax.random.permutation(jax.random.fold_in(own, 1), rows)]
    rotation = jax.random.randint(jax.random.fold_in(own, 2), (rows, 1), 0, top)
    return jnp.take_along_axis(table, (jnp.arange(top)[None, :] + rotation) % top, axis=1)


def shares(amount, total, most, lean, full):
    portions = [(1 << 20) // math.isqrt(standing ** lean) + 1 for standing in range(1, amount + 1)]
    largest = most if full else min(most, max(-(-total // amount), total * portions[0] // sum(portions)))
    least = 1 if total - largest >= amount - 1 else 0
    counts, rest = [largest] + [least] * (amount - 1), total - largest - least * (amount - 1)
    while rest > 0:
        movable = [i for i in range(1, amount) if counts[i] < largest] or [i for i in range(1, amount) if counts[i] < most]
        pool, budget = sum([portions[i] for i in movable]), rest
        for i in movable:
            addition = min(most - counts[i], max(1, budget * portions[i] // pool), rest)
            counts[i] = counts[i] + addition
            rest = rest - addition
    return np.array(counts)


def centred(own_key, extent, spread, limit, split=(), kind=jnp.bfloat16):
    drawn = jax.random.normal(own_key, extent, jnp.float32) * spread
    if len(split) > 0:
        drawn = block_scale(own_key, extent, split, -0.22, 0.18) * drawn
    return jnp.clip(drawn, min=-limit, max=limit).astype(kind)


def setup_inputs(seed: int = 0) -> dict:
    splits = jax.random.split(jax.random.key(seed), 7)
    tokens = centred(splits[0], (TOKENS, D), 1.0, 6.0, ((0, 16), (1, 2)))
    cotangent = centred(splits[1], (TOKENS, D), 1.0, 6.0, ((0, 16), (1, 2)))
    routes_keys = jax.random.split(jax.random.fold_in(splits[2], 1), TOKENS // TOK_DEV)
    routes_turns = jax.random.permutation(jax.random.fold_in(splits[2], 3), TOKENS // TOK_DEV)
    routes = jax.vmap(lambda own, number: assign_block(jax.random.fold_in(splits[2], 2), own, number, TOK_DEV, EXPERTS, TOPK, CAP, 2))(routes_keys, routes_turns).reshape((TOKENS, TOPK))
    route_weights = jnp.clip(0.05 + 0.45 * jax.random.uniform(splits[3], (TOKENS, TOPK), jnp.float32) ** block_scale(splits[3], (TOKENS, TOPK), ((0, 16),), -0.2, 0.2), 0.05, 0.5)
    gate_up = centred(splits[4], (EXPERTS * SPLIT, D, 2 * (FF // SPLIT)), D ** -0.5, 0.0625, ((0, 16), (1, 2)))
    down_proj = centred(splits[5], (EXPERTS * SPLIT, FF // SPLIT, D), FF ** -0.5, 0.125, ((0, 16), (2, 2)))
    return dict(tokens=tokens, cotangent=cotangent, routes=routes, route_weights=route_weights, gate_up=gate_up, down_proj=down_proj)


def slot_table(routes):
    count = TOK_DEV * TOPK
    blocks = routes.reshape(N_EP, count)
    order = jnp.arange(count, dtype=jnp.int32)
    earlier = order[None, :] < order[:, None]
    same = blocks[:, :, None] == blocks[:, None, :]
    rank_of = jnp.sum((same & earlier[None]).astype(jnp.int32), axis=2)
    source = jnp.arange(N_EP, dtype=jnp.int32)[:, None]
    return (blocks * (N_EP * CAP) + source * CAP + rank_of).reshape(-1).astype(jnp.int32)


def rounded_sum(parts):
    kept = lax.optimization_barrier(parts.astype(jnp.bfloat16))
    return jnp.sum(kept.astype(jnp.float32), axis=0)


def expert_pass(x_rows, d_rows, w_pair, w_down):
    rows = x_rows.shape[0]
    width = D // N_DP
    share = w_down.shape[0]
    x_split = x_rows.astype(jnp.float32).reshape(rows, N_DP, width)
    w_split = w_pair.astype(jnp.float32).reshape(N_DP, width, 2 * share)
    pre = rounded_sum(jnp.einsum("rjd,jdf->jrf", x_split, w_split))
    gate = pre[:, :share]
    upper = pre[:, share:]
    sigmoid_g = jax.nn.sigmoid(gate)
    silu_g = gate * sigmoid_g
    hidden = (silu_g * upper).astype(jnp.bfloat16)
    out_rows = jnp.dot(hidden, w_down, preferred_element_type=jnp.float32).astype(jnp.bfloat16)
    d_split = d_rows.astype(jnp.float32).reshape(rows, N_DP, width)
    down_split = w_down.astype(jnp.float32).reshape(share, N_DP, width)
    grad_hidden = rounded_sum(jnp.einsum("rjd,fjd->jrf", d_split, down_split))
    grad_gate = (grad_hidden * upper * sigmoid_g * (1.0 + gate * (1.0 - sigmoid_g))).astype(jnp.bfloat16)
    grad_up = (grad_hidden * silu_g).astype(jnp.bfloat16)
    grad_pair = jnp.concatenate([grad_gate, grad_up], axis=1)
    weight_grad = lax.dot_general(x_rows, grad_pair, (((0,), (0,)), ((), ())), preferred_element_type=jnp.float32).astype(jnp.bfloat16)
    dx_rows = lax.dot_general(grad_pair, w_pair, (((1,), (1,)), ((), ())), preferred_element_type=jnp.float32).astype(jnp.bfloat16)
    return out_rows, dx_rows, weight_grad


def reference(tokens, cotangent, routes, route_weights, gate_up, down_proj):
    slot_ids = slot_table(routes)
    total = EXPERTS * N_EP * CAP
    token_of = (jnp.arange(TOKENS * TOPK, dtype=jnp.int32) // TOPK).astype(jnp.int32)
    weight_flat = route_weights.reshape(-1)
    x_pairs = tokens[token_of]
    d_pairs = (weight_flat[:, None] * cotangent[token_of].astype(jnp.float32)).astype(jnp.bfloat16)
    x_buf = jnp.zeros((total, D), jnp.bfloat16).at[slot_ids].set(x_pairs).reshape(EXPERTS, N_EP * CAP, D)
    d_buf = jnp.zeros((total, D), jnp.bfloat16).at[slot_ids].set(d_pairs).reshape(EXPERTS, N_EP * CAP, D)

    def one_share(operands):
        index, w_pair, w_down = operands
        owner = (index // SPLIT).astype(jnp.int32)
        return expert_pass(x_buf[owner], d_buf[owner], w_pair, w_down)

    indices = jnp.arange(EXPERTS * SPLIT, dtype=jnp.int32)
    out_parts, dx_parts, gate_up_grad = lax.map(one_share, (indices, gate_up, down_proj))
    out_buf = jnp.sum(out_parts.astype(jnp.float32).reshape(EXPERTS, SPLIT, N_EP * CAP, D), axis=1)
    dx_buf = jnp.sum(dx_parts.astype(jnp.float32).reshape(EXPERTS, SPLIT, N_EP * CAP, D), axis=1)
    out_pairs = out_buf.reshape(total, D)[slot_ids]
    dx_pairs = dx_buf.reshape(total, D)[slot_ids]
    mixed = jnp.sum((weight_flat[:, None] * out_pairs).reshape(TOKENS, TOPK, D), axis=1).astype(jnp.bfloat16)
    token_grad = jnp.sum(dx_pairs.reshape(TOKENS, TOPK, D), axis=1).astype(jnp.bfloat16)
    return mixed, token_grad, gate_up_grad
```

```python
import jax
import jax.numpy as jnp
from jax import lax
from jax.sharding import PartitionSpec as P

FF = 2048
PIECE = 1024


def dp_sum(part, dp_count):
    sent = part.astype(jnp.bfloat16)
    if dp_count != 2:
        return lax.psum(sent, "dp").astype(jnp.float32)
    other = lax.ppermute(sent, "dp", [(0, 1), (1, 0)])
    return sent.astype(jnp.float32) + other.astype(jnp.float32)


def on_device(tokens, cotangent, routes, route_weights, gate_up, down_proj):
    tok_rows, width = tokens.shape
    hidden_units = down_proj.shape[1]
    split = FF // hidden_units
    ep_count = lax.axis_size("ep")
    dp_count = lax.axis_size("dp")
    experts = ep_count // split
    expert = lax.axis_index("ep") // split
    table = jnp.sum(
        jnp.where(
            routes[:, :, None] == jnp.arange(experts, dtype=jnp.int32)[None, None, :],
            route_weights[:, :, None],
            0.0,
        ),
        axis=1,
    )
    high = lax.reduce_precision(table, 8, 7)
    rest = table - high
    middle = lax.reduce_precision(rest, 8, 7)
    low = rest - middle
    packed = jnp.concatenate([high, middle, low], axis=1).astype(jnp.bfloat16)
    packed = jnp.pad(packed, ((0, 0), (0, -packed.shape[1] % 128)))
    first = lax.all_gather(jnp.concatenate([tokens, packed], axis=1), "ep", axis=0, tiled=True)
    d_all = lax.all_gather(cotangent, "ep", axis=0, tiled=True)
    x_all = first[:, :width]
    parts = first[:, width:].astype(jnp.float32)
    mine = jnp.arange(experts, dtype=jnp.int32)[None, :] == expert
    weight = jnp.sum(
        jnp.where(
            mine,
            parts[:, :experts]
            + (parts[:, experts : 2 * experts] + parts[:, 2 * experts : 3 * experts]),
            0.0,
        ),
        axis=1,
        keepdims=True,
    )
    named = weight > 0.0
    x_rows = jnp.where(named, x_all, jnp.zeros_like(x_all))
    d_rows = (weight * d_all.astype(jnp.float32)).astype(jnp.bfloat16)
    w_pair = gate_up[0]
    w_down = down_proj[0]
    piece = min(PIECE, hidden_units)
    pre = [
        dp_sum(
            jnp.dot(x_rows, w_pair[:, at : at + piece], preferred_element_type=jnp.float32),
            dp_count,
        )
        for at in range(0, 2 * hidden_units, piece)
    ]
    back = [
        dp_sum(
            lax.dot_general(
                d_rows,
                w_down[at : at + piece],
                (((1,), (1,)), ((), ())),
                preferred_element_type=jnp.float32,
            ),
            dp_count,
        )
        for at in range(0, hidden_units, piece)
    ]
    gate = jnp.concatenate(pre[: len(back)], axis=1)
    upper = jnp.concatenate(pre[len(back) :], axis=1)
    grad_hidden = jnp.concatenate(back, axis=1)
    sigmoid_g = jax.nn.sigmoid(gate)
    silu_g = gate * sigmoid_g
    hidden = (silu_g * upper).astype(jnp.bfloat16)
    grad_gate = (grad_hidden * upper * sigmoid_g * (1.0 + gate * (1.0 - sigmoid_g))).astype(
        jnp.bfloat16
    )
    grad_up = (grad_hidden * silu_g).astype(jnp.bfloat16)
    grad_pair = jnp.concatenate([grad_gate, grad_up], axis=1)
    out_rows = (weight * jnp.dot(hidden, w_down, preferred_element_type=jnp.float32)).astype(
        jnp.bfloat16
    )
    mixed = lax.psum_scatter(out_rows, "ep", scatter_dimension=0, tiled=True)
    dx_rows = lax.dot_general(
        grad_pair, w_pair, (((1,), (1,)), ((), ())), preferred_element_type=jnp.float32
    ).astype(jnp.bfloat16)
    token_grad = lax.psum_scatter(dx_rows, "ep", scatter_dimension=0, tiled=True)
    weight_grad = lax.dot_general(
        x_rows, grad_pair, (((0,), (0,)), ((), ())), preferred_element_type=jnp.float32
    ).astype(jnp.bfloat16)
    return (mixed, token_grad, weight_grad[None])


def solution(mesh):
    return jax.shard_map(
        on_device,
        mesh=mesh,
        in_specs=(
            P("ep", "dp"),
            P("ep", "dp"),
            P("ep", None),
            P("ep", None),
            P("ep", "dp", None),
            P("ep", None, "dp"),
        ),
        out_specs=(P("ep", "dp"), P("ep", "dp"), P("ep", "dp", None)),
        check_vma=False,
    )
```

```python
import jax
import jax.numpy as jnp
from jax import lax
from jax.experimental import pallas as pl
from jax.experimental.pallas import tpu as pltpu
from jax.sharding import PartitionSpec as P

FF = 2048
PIECE = 1024


def dp_sum(part, dp_count):
    sent = part.astype(jnp.bfloat16)
    if dp_count != 2:
        return lax.psum(sent, "dp").astype(jnp.float32)
    other = lax.ppermute(sent, "dp", [(0, 1), (1, 0)])
    return sent.astype(jnp.float32) + other.astype(jnp.float32)


def from_partner(block, offset, ep_count):
    return lax.ppermute(block, "ep", [(i, i ^ offset) for i in range(ep_count)])


def far_offsets(ep_count):
    return range(4, ep_count, 4)


def gather_far(block, ep_count):
    return jnp.concatenate(
        [block] + [from_partner(block, offset, ep_count) for offset in far_offsets(ep_count)]
    )


def gather_near(rows, ep_count):
    for offset in (2, 1):
        rows = jnp.concatenate([rows, from_partner(rows, offset, ep_count)])
    return rows


def sum_near(kept, offset, ep_count, beside):
    half = kept.shape[0] // 2
    sent, beside = lax.optimization_barrier((kept[half:].astype(jnp.bfloat16), beside))
    other = from_partner(sent, offset, ep_count)
    return (lambda: kept[:half].astype(jnp.float32) + other.astype(jnp.float32)), beside


def sum_far(kept, ep_count, beside):
    size = kept.shape[0] // (ep_count // 4)
    sent, beside = lax.optimization_barrier((kept.astype(jnp.bfloat16), beside))
    others = [
        from_partner(sent[number * size : (number + 1) * size], offset, ep_count)
        for number, offset in enumerate(far_offsets(ep_count), 1)
    ]

    def finish():
        total = kept[:size]
        for other in others:
            total = total + other.astype(jnp.float32)
        return total.astype(jnp.bfloat16)

    return finish, beside


def grad_kernel(x_ref, g_ref, *refs):
    o_ref = refs[-1]
    columns = o_ref.shape[1]
    step = min(1024, columns)
    for at in range(0, columns, step):
        o_ref[:, at : at + step] = jnp.dot(
            x_ref[...], g_ref[:, at : at + step], preferred_element_type=jnp.float32
        ).astype(o_ref.dtype)


def grad_part(x_turned, pair, start, count, block, whole):
    width, rows = x_turned.shape
    columns = pair.shape[1]
    given = () if whole is None else (whole,)
    return pl.pallas_call(
        grad_kernel,
        out_shape=jax.ShapeDtypeStruct((width, columns), jnp.bfloat16),
        grid=(count,),
        in_specs=[
            pl.BlockSpec((block, rows), lambda i: (i + start, 0)),
            pl.BlockSpec((rows, columns), lambda i: (0, 0)),
        ]
        + [pl.BlockSpec(memory_space=pl.ANY)] * len(given),
        out_specs=pl.BlockSpec((block, columns), lambda i: (i + start, 0)),
        input_output_aliases={2: 0} if given else {},
        cost_estimate=pl.CostEstimate(
            flops=2 * count * block * rows * columns,
            bytes_accessed=2 * count * block * (columns + rows) + 2 * rows * columns,
            transcendentals=0,
        ),
        compiler_params=pltpu.CompilerParams(vmem_limit_bytes=32 * 2**20),
    )(x_turned, pair, *given)


def on_device(tokens, cotangent, routes, route_weights, gate_up, down_proj):
    tok_rows, width = tokens.shape
    hidden_units = down_proj.shape[1]
    split = FF // hidden_units
    ep_count = lax.axis_size("ep")
    dp_count = lax.axis_size("dp")
    experts = ep_count // split
    expert = lax.axis_index("ep") // split
    table = jnp.sum(
        jnp.where(
            routes[:, :, None] == jnp.arange(experts, dtype=jnp.int32)[None, None, :],
            route_weights[:, :, None],
            0.0,
        ),
        axis=1,
    )
    high = lax.reduce_precision(table, 8, 7)
    rest = table - high
    middle = lax.reduce_precision(rest, 8, 7)
    low = rest - middle
    packed = jnp.concatenate([high, middle, low], axis=1).astype(jnp.bfloat16)
    packed = jnp.pad(packed, ((0, 0), (0, -packed.shape[1] % 128)))
    first = gather_far(jnp.concatenate([tokens, packed], axis=1), ep_count)
    first, cotangent = lax.optimization_barrier((first, cotangent))
    first = gather_near(first, ep_count)
    d_far = gather_far(cotangent, ep_count)
    x_all = first[:, :width]
    parts = first[:, width:].astype(jnp.float32)
    mine = jnp.arange(experts, dtype=jnp.int32)[None, :] == expert
    weight = jnp.sum(
        jnp.where(
            mine,
            parts[:, :experts]
            + (parts[:, experts : 2 * experts] + parts[:, 2 * experts : 3 * experts]),
            0.0,
        ),
        axis=1,
        keepdims=True,
    )
    named = weight > 0.0
    x_rows = jnp.where(named, x_all, jnp.zeros_like(x_all))
    w_pair = gate_up[0]
    w_down = down_proj[0]
    piece = min(PIECE, hidden_units)
    starts = list(range(0, 2 * hidden_units, piece))
    d_far, x_rows = lax.optimization_barrier((d_far, x_rows))
    d_near = jnp.concatenate([d_far, from_partner(d_far, 2, ep_count)])

    def pre_piece(at, x):
        return jnp.dot(
            x, w_pair[:, at : at + piece], preferred_element_type=jnp.float32
        ).astype(jnp.bfloat16)

    early = len(starts) // 2
    terms = [pre_piece(at, x_rows) for at in starts[:early]]
    d_near, x_late = lax.optimization_barrier((d_near, x_rows))
    d_all = jnp.concatenate([d_near, from_partner(d_near, 1, ep_count)])
    terms += [pre_piece(at, x_late) for at in starts[early:]]
    pre = [dp_sum(term, dp_count) for term in terms]
    d_rows = (weight * d_all.astype(jnp.float32)).astype(jnp.bfloat16)
    back = [
        dp_sum(
            lax.dot_general(
                d_rows,
                w_down[at : at + piece],
                (((1,), (1,)), ((), ())),
                preferred_element_type=jnp.float32,
            ),
            dp_count,
        )
        for at in range(0, hidden_units, piece)
    ]
    gate = jnp.concatenate(pre[: len(back)], axis=1)
    upper = jnp.concatenate(pre[len(back) :], axis=1)
    grad_hidden = jnp.concatenate(back, axis=1)
    sigmoid_g = jax.nn.sigmoid(gate)
    silu_g = gate * sigmoid_g
    hidden = (silu_g * upper).astype(jnp.bfloat16)
    grad_gate = (grad_hidden * upper * sigmoid_g * (1.0 + gate * (1.0 - sigmoid_g))).astype(
        jnp.bfloat16
    )
    grad_up = (grad_hidden * silu_g).astype(jnp.bfloat16)
    grad_pair = jnp.concatenate([grad_gate, grad_up], axis=1)
    out_rows = (weight * jnp.dot(hidden, w_down, preferred_element_type=jnp.float32)).astype(
        jnp.bfloat16
    )
    strip = width // 4 if width % 512 == 0 else width // 2

    def dx_strips(pair, begin, end):
        return [
            lax.dot_general(
                pair,
                w_pair[at : at + strip],
                (((1,), (1,)), ((), ())),
                preferred_element_type=jnp.float32,
            ).astype(jnp.bfloat16)
            for at in range(begin, end, strip)
        ]

    finish, pair = sum_near(out_rows, 1, ep_count, grad_pair)
    strips = dx_strips(pair, 0, strip)
    finish, pair = sum_near(finish(), 2, ep_count, pair)
    strips += dx_strips(pair, strip, width // 2)
    finish, pair = sum_far(finish(), ep_count, pair)
    strips += dx_strips(pair, width // 2, width)
    mixed = finish()
    dx_rows = jnp.concatenate(strips, axis=1)
    block = 256 if width % 256 == 0 else width
    blocks = width // block
    cuts = (0, blocks // 4, blocks * 9 // 16, blocks)
    x_turned = x_rows.T
    whole = None
    finish, x_turned = sum_near(dx_rows, 1, ep_count, x_turned)
    for number in range(3):
        count = cuts[number + 1] - cuts[number]
        if count > 0:
            whole = grad_part(x_turned, grad_pair, cuts[number], count, block, whole)
        if number == 0:
            finish, x_turned = sum_near(finish(), 2, ep_count, x_turned)
        if number == 1:
            finish, x_turned = sum_far(finish(), ep_count, x_turned)
    token_grad = finish()
    weight_grad = whole
    return (mixed, token_grad, weight_grad[None])


def solution(mesh):
    return jax.shard_map(
        on_device,
        mesh=mesh,
        in_specs=(
            P("ep", "dp"),
            P("ep", "dp"),
            P("ep", None),
            P("ep", None),
            P("ep", "dp", None),
            P("ep", None, "dp"),
        ),
        out_specs=(P("ep", "dp"), P("ep", "dp"), P("ep", "dp", None)),
        check_vma=False,
    )
```

```python
import jax
import jax.numpy as jnp
from jax import lax
from jax.experimental import pallas as pl
from jax.experimental.pallas import tpu as pltpu
from jax.sharding import PartitionSpec as P

FF = 2048


def dp_sum(part, dp_count):
    sent = part.astype(jnp.bfloat16)
    if dp_count != 2:
        return lax.psum(sent, "dp").astype(jnp.float32)
    other = lax.ppermute(sent, "dp", [(0, 1), (1, 0)])
    return sent.astype(jnp.float32) + other.astype(jnp.float32)


def from_partner(block, offset, ep_count):
    return lax.ppermute(block, "ep", [(i, i ^ offset) for i in range(ep_count)])


def far_offsets(ep_count):
    return range(4, ep_count, 4)


def gather_far(block, ep_count):
    return jnp.concatenate(
        [block] + [from_partner(block, offset, ep_count) for offset in far_offsets(ep_count)]
    )


def gather_near(rows, ep_count):
    for offset in (2, 1):
        rows = jnp.concatenate([rows, from_partner(rows, offset, ep_count)])
    return rows


def sum_near(kept, offset, ep_count, beside):
    half = kept.shape[0] // 2
    sent, beside = lax.optimization_barrier((kept[half:].astype(jnp.bfloat16), beside))
    other = from_partner(sent, offset, ep_count)
    return (lambda: kept[:half].astype(jnp.float32) + other.astype(jnp.float32)), beside


def sum_far(kept, ep_count, beside):
    size = kept.shape[0] // (ep_count // 4)
    sent, beside = lax.optimization_barrier((kept.astype(jnp.bfloat16), beside))
    others = [
        from_partner(sent[number * size : (number + 1) * size], offset, ep_count)
        for number, offset in enumerate(far_offsets(ep_count), 1)
    ]

    def finish():
        total = kept[:size]
        for other in others:
            total = total + other.astype(jnp.float32)
        return total.astype(jnp.bfloat16)

    return finish, beside


def grad_kernel(x_ref, g_ref, *refs):
    o_ref = refs[-1]
    o_ref[...] = jnp.dot(
        x_ref[...], g_ref[...], preferred_element_type=jnp.float32
    ).astype(o_ref.dtype)


def grad_part(x_turned, pair, turn, start, count, block, whole):
    width, rows = x_turned.shape
    piece = pair.shape[1] // 2
    given = () if whole is None else (whole,)
    return pl.pallas_call(
        grad_kernel,
        out_shape=jax.ShapeDtypeStruct((width, 4 * piece), jnp.bfloat16),
        grid=(2, count),
        in_specs=[
            pl.BlockSpec((block, rows), lambda c, i: (i + start, 0)),
            pl.BlockSpec((rows, piece), lambda c, i: (0, c)),
        ]
        + [pl.BlockSpec(memory_space=pl.ANY)] * len(given),
        out_specs=pl.BlockSpec((block, piece), lambda c, i: (i + start, 2 * c + turn)),
        input_output_aliases={2: 0} if given else {},
        cost_estimate=pl.CostEstimate(
            flops=4 * count * block * rows * piece,
            bytes_accessed=4 * count * block * (piece + rows) + 4 * rows * piece,
            transcendentals=0,
        ),
        compiler_params=pltpu.CompilerParams(vmem_limit_bytes=32 * 2**20),
    )(x_turned, pair, *given)


def activate(gate, upper, grad_hidden):
    sigmoid_g = jax.nn.sigmoid(gate)
    silu_g = gate * sigmoid_g
    hidden = (silu_g * upper).astype(jnp.bfloat16)
    grad_gate = (grad_hidden * upper * sigmoid_g * (1.0 + gate * (1.0 - sigmoid_g))).astype(
        jnp.bfloat16
    )
    grad_up = (grad_hidden * silu_g).astype(jnp.bfloat16)
    return hidden, grad_gate, grad_up


def on_device(tokens, cotangent, routes, route_weights, gate_up, down_proj):
    tok_rows, width = tokens.shape
    hidden_units = down_proj.shape[1]
    split = FF // hidden_units
    ep_count = lax.axis_size("ep")
    dp_count = lax.axis_size("dp")
    experts = ep_count // split
    expert = lax.axis_index("ep") // split
    table = jnp.sum(
        jnp.where(
            routes[:, :, None] == jnp.arange(experts, dtype=jnp.int32)[None, None, :],
            route_weights[:, :, None],
            0.0,
        ),
        axis=1,
    )
    high = lax.reduce_precision(table, 8, 7)
    rest = table - high
    middle = lax.reduce_precision(rest, 8, 7)
    low = rest - middle
    packed = jnp.concatenate([high, middle, low], axis=1).astype(jnp.bfloat16)
    packed = jnp.pad(packed, ((0, 0), (0, -packed.shape[1] % 128)))
    first = gather_far(jnp.concatenate([tokens, packed], axis=1), ep_count)
    first, cotangent = lax.optimization_barrier((first, cotangent))
    first = gather_near(first, ep_count)
    d_far = gather_far(cotangent, ep_count)
    x_all = first[:, :width]
    parts = first[:, width:].astype(jnp.float32)
    mine = jnp.arange(experts, dtype=jnp.int32)[None, :] == expert
    weight = jnp.sum(
        jnp.where(
            mine,
            parts[:, :experts]
            + (parts[:, experts : 2 * experts] + parts[:, 2 * experts : 3 * experts]),
            0.0,
        ),
        axis=1,
        keepdims=True,
    )
    named = weight > 0.0
    x_rows = jnp.where(named, x_all, jnp.zeros_like(x_all))
    w_pair = gate_up[0]
    w_down = down_proj[0]
    piece = hidden_units // 2
    d_far, x_rows = lax.optimization_barrier((d_far, x_rows))
    d_near = jnp.concatenate([d_far, from_partner(d_far, 2, ep_count)])

    def pre_piece(at, x):
        return jnp.dot(
            x, w_pair[:, at : at + piece], preferred_element_type=jnp.float32
        ).astype(jnp.bfloat16)

    def back_piece(at, d):
        return lax.dot_general(
            d, w_down[at : at + piece], (((1,), (1,)), ((), ())), preferred_element_type=jnp.float32
        ).astype(jnp.bfloat16)

    gate_a = dp_sum(pre_piece(0, x_rows), dp_count)
    d_near, x_next = lax.optimization_barrier((d_near, x_rows))
    d_all = jnp.concatenate([d_near, from_partner(d_near, 1, ep_count)])
    upper_a = dp_sum(pre_piece(hidden_units, x_next), dp_count)
    d_rows = (weight * d_all.astype(jnp.float32)).astype(jnp.bfloat16)
    gate_a, x_next = lax.optimization_barrier((gate_a, x_next))
    gate_b = dp_sum(pre_piece(piece, x_next), dp_count)
    upper_a, d_rows = lax.optimization_barrier((upper_a, d_rows))
    back_a = dp_sum(back_piece(0, d_rows), dp_count)
    gate_b, x_next = lax.optimization_barrier((gate_b, x_next))
    upper_b = dp_sum(pre_piece(hidden_units + piece, x_next), dp_count)
    back_a, d_rows = lax.optimization_barrier((back_a, d_rows))
    last = back_piece(piece, d_rows)
    last, gate_a, upper_a, back_a = lax.optimization_barrier((last, gate_a, upper_a, back_a))
    back_b = dp_sum(last, dp_count)

    def dx_term(grad, at):
        return lax.dot_general(
            grad,
            w_pair[:, at : at + piece],
            (((1,), (1,)), ((), ())),
            preferred_element_type=jnp.float32,
        )

    block = 256 if width % 256 == 0 else width
    blocks = width // block
    x_turned = x_rows.T
    hidden_a, grad_gate, grad_up = activate(gate_a, upper_a, back_a)
    pair_a = jnp.concatenate([grad_gate, grad_up], axis=1)
    dx_sum = dx_term(grad_gate, 0) + dx_term(grad_up, hidden_units)
    out_sum = jnp.dot(hidden_a, w_down[:piece], preferred_element_type=jnp.float32)
    whole = None
    if blocks > 1:
        whole = grad_part(x_turned, pair_a, 0, 0, blocks // 2, block, whole)
    dx_sum, out_sum, gate_b, x_turned = lax.optimization_barrier(
        (dx_sum, out_sum, gate_b, x_turned)
    )
    hidden_b, grad_gate, grad_up = activate(gate_b, upper_b, back_b)
    pair_b = jnp.concatenate([grad_gate, grad_up], axis=1)
    out_sum = out_sum + jnp.dot(hidden_b, w_down[piece:], preferred_element_type=jnp.float32)
    out_rows = (weight * out_sum).astype(jnp.bfloat16)
    finish, grad_gate = sum_near(out_rows, 1, ep_count, grad_gate)
    dx_sum = dx_sum + dx_term(grad_gate, piece)
    finish, grad_up = sum_near(finish(), 2, ep_count, grad_up)
    dx_rows = (dx_sum + dx_term(grad_up, hidden_units + piece)).astype(jnp.bfloat16)
    finish_out, x_turned = sum_far(finish(), ep_count, x_turned)
    finish, x_turned = sum_near(dx_rows, 1, ep_count, x_turned)
    whole = grad_part(x_turned, pair_a, 0, blocks // 2, blocks - blocks // 2, block, whole)
    finish, x_turned = sum_near(finish(), 2, ep_count, x_turned)
    early = blocks * 3 // 7
    if early > 0:
        whole = grad_part(x_turned, pair_b, 1, 0, early, block, whole)
    finish, x_turned = sum_far(finish(), ep_count, x_turned)
    weight_grad = grad_part(x_turned, pair_b, 1, early, blocks - early, block, whole)
    mixed = finish_out()
    token_grad = finish()
    return (mixed, token_grad, weight_grad[None])


def solution(mesh):
    return jax.shard_map(
        on_device,
        mesh=mesh,
        in_specs=(
            P("ep", "dp"),
            P("ep", "dp"),
            P("ep", None),
            P("ep", None),
            P("ep", "dp", None),
            P("ep", None, "dp"),
        ),
        out_specs=(P("ep", "dp"), P("ep", "dp"), P("ep", "dp", None)),
        check_vma=False,
    )
```

```python
import jax
import jax.numpy as jnp
from jax import lax
from jax.experimental import pallas as pl
from jax.experimental.pallas import tpu as pltpu
from jax.sharding import PartitionSpec as P

FF = 2048
PIECE = 1024


def dp_sum(part, dp_count):
    sent = part.astype(jnp.bfloat16)
    if dp_count != 2:
        return lax.psum(sent, "dp").astype(jnp.float32)
    other = lax.ppermute(sent, "dp", [(0, 1), (1, 0)])
    return sent.astype(jnp.float32) + other.astype(jnp.float32)


def from_partner(block, offset, ep_count):
    return lax.ppermute(block, "ep", [(i, i ^ offset) for i in range(ep_count)])


def far_offsets(ep_count):
    return range(4, ep_count, 4)


def gather_far(block, ep_count):
    return jnp.concatenate(
        [block] + [from_partner(block, offset, ep_count) for offset in far_offsets(ep_count)]
    )


def gather_near(rows, ep_count):
    for offset in (2, 1):
        rows = jnp.concatenate([rows, from_partner(rows, offset, ep_count)])
    return rows


def sum_near(kept, offset, ep_count, beside):
    half = kept.shape[0] // 2
    sent, beside = lax.optimization_barrier((kept[half:].astype(jnp.bfloat16), beside))
    other = from_partner(sent, offset, ep_count)
    return (lambda: kept[:half].astype(jnp.float32) + other.astype(jnp.float32)), beside


def sum_far(kept, ep_count, beside):
    size = kept.shape[0] // (ep_count // 4)
    sent, beside = lax.optimization_barrier((kept.astype(jnp.bfloat16), beside))
    others = [
        from_partner(sent[number * size : (number + 1) * size], offset, ep_count)
        for number, offset in enumerate(far_offsets(ep_count), 1)
    ]

    def finish():
        total = kept[:size]
        for other in others:
            total = total + other.astype(jnp.float32)
        return total.astype(jnp.bfloat16)

    return finish, beside


def grad_kernel(x_ref, g_ref, *refs):
    o_ref = refs[-1]
    columns = o_ref.shape[1]
    step = min(1024, columns)
    for at in range(0, columns, step):
        o_ref[:, at : at + step] = jnp.dot(
            x_ref[...], g_ref[:, at : at + step], preferred_element_type=jnp.float32
        ).astype(o_ref.dtype)


def grad_part(x_turned, pair, start, count, block, whole):
    width, rows = x_turned.shape
    columns = pair.shape[1]
    given = () if whole is None else (whole,)
    return pl.pallas_call(
        grad_kernel,
        out_shape=jax.ShapeDtypeStruct((width, columns), jnp.bfloat16),
        grid=(count,),
        in_specs=[
            pl.BlockSpec((block, rows), lambda i: (i + start, 0)),
            pl.BlockSpec((rows, columns), lambda i: (0, 0)),
        ]
        + [pl.BlockSpec(memory_space=pl.ANY)] * len(given),
        out_specs=pl.BlockSpec((block, columns), lambda i: (i + start, 0)),
        input_output_aliases={2: 0} if given else {},
        cost_estimate=pl.CostEstimate(
            flops=2 * count * block * rows * columns,
            bytes_accessed=2 * count * block * (columns + rows) + 2 * rows * columns,
            transcendentals=0,
        ),
        compiler_params=pltpu.CompilerParams(vmem_limit_bytes=32 * 2**20),
    )(x_turned, pair, *given)


def on_device(tokens, cotangent, routes, route_weights, gate_up, down_proj):
    tok_rows, width = tokens.shape
    hidden_units = down_proj.shape[1]
    split = FF // hidden_units
    ep_count = lax.axis_size("ep")
    dp_count = lax.axis_size("dp")
    experts = ep_count // split
    expert = lax.axis_index("ep") // split
    table = jnp.sum(
        jnp.where(
            routes[:, :, None] == jnp.arange(experts, dtype=jnp.int32)[None, None, :],
            route_weights[:, :, None],
            0.0,
        ),
        axis=1,
    )
    high = lax.reduce_precision(table, 8, 7)
    rest = table - high
    middle = lax.reduce_precision(rest, 8, 7)
    low = rest - middle
    packed = jnp.concatenate([high, middle, low], axis=1).astype(jnp.bfloat16)
    packed = jnp.pad(packed, ((0, 0), (0, -packed.shape[1] % 128)))
    first = gather_far(jnp.concatenate([tokens, packed], axis=1), ep_count)
    first, cotangent = lax.optimization_barrier((first, cotangent))
    first = gather_near(first, ep_count)
    d_far = gather_far(cotangent, ep_count)
    x_all = first[:, :width]
    parts = first[:, width:].astype(jnp.float32)
    mine = jnp.arange(experts, dtype=jnp.int32)[None, :] == expert
    weight = jnp.sum(
        jnp.where(
            mine,
            parts[:, :experts]
            + (parts[:, experts : 2 * experts] + parts[:, 2 * experts : 3 * experts]),
            0.0,
        ),
        axis=1,
        keepdims=True,
    )
    named = weight > 0.0
    x_rows = jnp.where(named, x_all, jnp.zeros_like(x_all))
    w_pair = gate_up[0]
    w_down = down_proj[0]
    piece = min(PIECE, hidden_units)
    starts = list(range(0, 2 * hidden_units, piece))
    d_far, x_rows = lax.optimization_barrier((d_far, x_rows))
    d_near = jnp.concatenate([d_far, from_partner(d_far, 2, ep_count)])

    def pre_piece(at, x):
        return jnp.dot(
            x, w_pair[:, at : at + piece], preferred_element_type=jnp.float32
        ).astype(jnp.bfloat16)

    early = len(starts) // 2
    terms = [pre_piece(at, x_rows) for at in starts[:early]]
    d_near, x_late = lax.optimization_barrier((d_near, x_rows))
    d_all = jnp.concatenate([d_near, from_partner(d_near, 1, ep_count)])
    terms += [pre_piece(at, x_late) for at in starts[early:]]
    pre = [dp_sum(term, dp_count) for term in terms]
    d_rows = (weight * d_all.astype(jnp.float32)).astype(jnp.bfloat16)
    back = [
        dp_sum(
            lax.dot_general(
                d_rows,
                w_down[at : at + piece],
                (((1,), (1,)), ((), ())),
                preferred_element_type=jnp.float32,
            ),
            dp_count,
        )
        for at in range(0, hidden_units, piece)
    ]
    gate = jnp.concatenate(pre[: len(back)], axis=1)
    upper = jnp.concatenate(pre[len(back) :], axis=1)
    grad_hidden = jnp.concatenate(back, axis=1)
    sigmoid_g = jax.nn.sigmoid(gate)
    silu_g = gate * sigmoid_g
    hidden = (silu_g * upper).astype(jnp.bfloat16)
    grad_gate = (grad_hidden * upper * sigmoid_g * (1.0 + gate * (1.0 - sigmoid_g))).astype(
        jnp.bfloat16
    )
    grad_up = (grad_hidden * silu_g).astype(jnp.bfloat16)
    grad_pair = jnp.concatenate([grad_gate, grad_up], axis=1)
    out_rows = (weight * jnp.dot(hidden, w_down, preferred_element_type=jnp.float32)).astype(
        jnp.bfloat16
    )
    strip = width // 2
    x_turned = x_rows.T

    def dx_strips(pair, begin, end):
        return [
            lax.dot_general(
                pair,
                w_pair[at : at + strip],
                (((1,), (1,)), ((), ())),
                preferred_element_type=jnp.float32,
            ).astype(jnp.bfloat16)
            for at in range(begin, end, strip)
        ]

    finish, pair = sum_near(out_rows, 1, ep_count, grad_pair)
    strips = dx_strips(pair, 0, strip)
    finish, pair = sum_near(finish(), 2, ep_count, pair)
    strips += dx_strips(pair, strip, width)
    finish_out, x_turned = sum_far(finish(), ep_count, x_turned)
    dx_rows = jnp.concatenate(strips, axis=1)
    block = 256 if width % 256 == 0 else width
    blocks = width // block
    cuts = (0, blocks // 4, blocks * 9 // 16, blocks)
    whole = None
    finish, x_turned = sum_near(dx_rows, 1, ep_count, x_turned)
    for number in range(3):
        count = cuts[number + 1] - cuts[number]
        if count > 0:
            whole = grad_part(x_turned, grad_pair, cuts[number], count, block, whole)
        if number == 0:
            finish, x_turned = sum_near(finish(), 2, ep_count, x_turned)
        if number == 1:
            finish, x_turned = sum_far(finish(), ep_count, x_turned)
    mixed = finish_out()
    token_grad = finish()
    weight_grad = whole
    return (mixed, token_grad, weight_grad[None])


def solution(mesh):
    return jax.shard_map(
        on_device,
        mesh=mesh,
        in_specs=(
            P("ep", "dp"),
            P("ep", "dp"),
            P("ep", None),
            P("ep", None),
            P("ep", "dp", None),
            P("ep", None, "dp"),
        ),
        out_specs=(P("ep", "dp"), P("ep", "dp"), P("ep", "dp", None)),
        check_vma=False,
    )
```
